32 devices in a mesh: grp: 2 (over y), seq: 4 (over z), ch: 2 (over x), sub: 2 (over core).
Axes of the slice: x: 2, y: 2, z: 4, core: 2. Of those that a mesh axis runs over, the one named last changes fastest.
Arguments:
- tokens: bfloat16 [8, 384, 4, 512], P('grp', ('ch', 'sub'), 'seq'), parts along dimension 0, may hold values from -6 to 6
- gate_scale: float32 [4, 384], P(None, ('ch', 'sub')), may hold values from -4 to 4
- gate_shift: float32 [4, 384], P(None, ('ch', 'sub')), may hold values from -4 to 4
- sequence_right_factor: bfloat16 [4, 512, 512], P('seq'), may hold values from -0.25 to 0.25
- sequence_left_factor: bfloat16 [512, 4, 4], P('seq'), may hold values from -3 to 3
- up_first: bfloat16 [2, 4, 1536, 384], P(None, None, ('ch', 'sub')), may hold values from -0.3125 to 0.3125
- up_second: bfloat16 [2, 1536, 4, 4], P(None, ('ch', 'sub')), may hold values from -3 to 3
- up_shift: float32 [2, 4, 1536], P(None, None, ('ch', 'sub')), may hold values from -3 to 3
- down_first: bfloat16 [384, 4, 1536], P(None, None, ('ch', 'sub')), may hold values from -0.15625 to 0.15625
- down_second: bfloat16 [384, 4, 4], P(('ch', 'sub')), may hold values from -3 to 3
- cotangent: bfloat16 [8, 384, 4, 512], P('grp', ('ch', 'sub'), 'seq'), parts along dimension 0, may hold values from -6 to 6
Outputs:
- layer_out: bfloat16 [8, 384, 4, 512], P('grp', ('ch', 'sub'), 'seq'), parts along dimension 0
- token_input_gradient: float32 [8, 384, 4, 512], P('grp', ('ch', 'sub'), 'seq'), parts along dimension 0
- right_factor_gradient: float32 [8, 512, 512], P(('grp', 'seq')), parts along dimension 0
- left_factor_gradient: float32 [1024, 4, 4], P(('grp', 'seq')), parts along dimension 0
- up_first_grad: float32 [4, 4, 1536, 384], P('grp', None, ('ch', 'sub')), parts along dimension 0
- down_first_grad: float32 [768, 4, 1536], P('grp', None, ('ch', 'sub')), parts along dimension 0
The draws below stay inside these ranges and needn't reach their ends.
There are 2 independent parts, one for each index of `grp`. The reference program is written for one: setup_inputs(seed, part) draws one part's arguments, and reference() takes and returns one part's arrays. A program takes and returns all parts, laid end to end along the dimension named above; an argument that names none is the same for every part. Nothing has to cross between parts.
All inputs are finite; a program needn't handle non-finite values.
Results may differ from the reference program's by a relative error of at most 0.017.
Values may be sent and summed in bfloat16 or wider, within the bound.
A program may use at most 128 MiB of HBM per device.

```python
import jax
import jax.numpy as jnp
from jax import lax

KB = 4
BS = 512
PB = 384
FQ = 1536
NB = 4
N_CH = 2
N_SUB = 2


def levels(stream_key, shape, split, least, top_value):
    def one(dim, shards_of):
        steps = jax.random.uniform(jax.random.fold_in(jax.random.fold_in(stream_key, 6), dim), (shards_of,), jnp.float32, least / len(split), top_value / len(split))
        return jnp.repeat(jnp.exp(steps), shape[dim] // shards_of).reshape((-1,) + (1,) * (len(shape) - dim - 1))

    level = one(*split[0])
    for cut in split[1:]:
        level = level * one(*cut)
    return level


def noise(own_key, shape, spread, limit, split=(), dtype=jnp.bfloat16):
    level = levels(own_key, shape, split, -0.22, 0.18) if split else 1.0
    drawn = jax.random.normal(own_key, shape, jnp.float32) * spread * level
    return jnp.minimum(jnp.maximum(drawn, -limit), limit).astype(dtype)


def setup_inputs(seed: int = 0, part: int = 0) -> dict:
    seeds = jax.random.split(jax.random.key(seed), 12)
    part_splits = jax.random.split(jax.random.fold_in(seeds[11], part), 12)
    tokens = noise(part_splits[0], (KB, PB, NB, BS), 1.0, 6.0, ((1, 4), (2, 4)))
    gate_scale = noise(seeds[1], (KB, PB), 1.0, 4.0, ((1, 4),), jnp.float32)
    gate_shift = noise(seeds[2], (KB, PB), 1.0, 4.0, ((1, 4),), jnp.float32)
    sequence_right_factor = noise(seeds[3], (NB, BS, BS), BS ** -0.5, 0.25, ((0, 4),))
    sequence_left_factor = noise(seeds[4], (BS, NB, NB), NB ** -0.5, 3.0, ((0, 4),))
    up_first = noise(seeds[5], (2, KB, FQ, PB), PB ** -0.5, 0.3125, ((2, 4),))
    up_second = noise(seeds[6], (2, FQ, KB, KB), KB ** -0.5, 3.0, ((1, 4),))
    up_shift = noise(seeds[7], (2, KB, FQ), 0.5, 3.0, ((2, 4),), jnp.float32)
    down_first = noise(seeds[8], (PB, KB, FQ), FQ ** -0.5, 0.15625, ((2, 4),))
    down_second = noise(seeds[9], (PB, KB, KB), KB ** -0.5, 3.0, ((0, 4),))
    cotangent = noise(part_splits[10], (KB, PB, NB, BS), 1.0, 6.0, ((1, 4), (2, 4)))
    return {"tokens": tokens, "gate_scale": gate_scale, "gate_shift": gate_shift, "sequence_right_factor": sequence_right_factor, "sequence_left_factor": sequence_left_factor, "up_first": up_first, "up_second": up_second, "up_shift": up_shift, "down_first": down_first, "down_second": down_second, "cotangent": cotangent}


top_precision = lax.Precision.HIGHEST

def rounded_values(value):
    return lax.optimization_barrier(value.astype(jnp.bfloat16)).astype(jnp.float32)

def gated_unit(stacked):
    return jax.nn.gelu(stacked[0]) * stacked[1]

def channel_block(block_in, block_cot, up_first, up_second, up_shift, down_first, down_second):
    groups = N_CH * N_SUB
    token_count = block_in.shape[-1]
    input_tokens = block_in.astype(jnp.float32)
    first_w = up_first.astype(jnp.float32)
    second_w = up_second.astype(jnp.float32)
    down_w = down_first.astype(jnp.float32)
    mix_w = down_second.astype(jnp.float32)
    lifted = jnp.einsum('gkqp,kpt->gkqt', first_w, input_tokens, precision=top_precision)
    stacked = jnp.einsum('gqjk,gkqt->gjqt', second_w, lifted, precision=top_precision) + up_shift[:, :, :, None]
    hidden = rounded_values(gated_unit(stacked))
    grouped_h = hidden.reshape(KB, groups, FQ // groups, token_count)
    grouped_v = down_w.reshape(PB, KB, groups, FQ // groups)
    partial_sums = rounded_values(jnp.einsum('rjaq,jaqt->arjt', grouped_v, grouped_h, precision=top_precision))
    reduced = lax.optimization_barrier(jnp.sum(partial_sums, axis=0))
    output = jnp.einsum('rkj,rjt->krt', mix_w, reduced, precision=top_precision)
    block_out = (input_tokens + output).astype(jnp.bfloat16)
    upstream = block_cot.astype(jnp.float32)
    down_cot = rounded_values(jnp.einsum('rkj,krt->jrt', mix_w, upstream, precision=top_precision))
    hidden_cot = jnp.einsum('rjq,jrt->jqt', down_w, down_cot, precision=top_precision)
    down_grad = jnp.einsum('jrt,jqt->rjq', down_cot, hidden, precision=top_precision)
    gate_pull = jax.vjp(gated_unit, stacked)[1]
    stacked_cot = gate_pull(hidden_cot)[0]
    lifted_cot = rounded_values(jnp.einsum('gqjk,gjqt->gkqt', second_w, stacked_cot, precision=top_precision))
    first_grad = jnp.einsum('gkqt,kpt->gkqp', lifted_cot, input_tokens, precision=top_precision)
    grouped_w = first_w.reshape(2, KB, groups, FQ // groups, PB)
    grouped_c = lifted_cot.reshape(2, KB, groups, FQ // groups, token_count)
    back_parts = rounded_values(jnp.einsum('gkaqp,gkaqt->akpt', grouped_w, grouped_c, precision=top_precision))
    input_cot = lax.optimization_barrier(jnp.sum(back_parts, axis=0))
    return (block_out, input_cot, first_grad, down_grad)

def reference(tokens, gate_scale, gate_shift, sequence_right_factor, sequence_left_factor, up_first, up_second, up_shift, down_first, down_second, cotangent):
    input_tokens = tokens.astype(jnp.float32)
    right_weight_matrix = sequence_right_factor.astype(jnp.float32)
    left_weight_matrix = sequence_left_factor.astype(jnp.float32)
    first_section = rounded_values(jnp.einsum('oaj,zuoj->zuoa', right_weight_matrix, input_tokens, precision=top_precision))
    sequence_mixed = rounded_values(jnp.einsum('hli,xoih->xolh', left_weight_matrix, first_section, precision=top_precision))
    gating = jax.nn.sigmoid(input_tokens * gate_scale[:, :, None, None] + gate_shift[:, :, None, None])
    seq_out = (input_tokens + gating * sequence_mixed).astype(jnp.bfloat16)

    def scan_step(partial_value, block_pair):
        block_out, input_cot, first_grad, down_grad = channel_block(block_pair[0], block_pair[1], up_first, up_second, up_shift, down_first, down_second)
        return ((partial_value[0] + first_grad, partial_value[1] + down_grad), (block_out, input_cot))
    blocks_in = jnp.transpose(seq_out, (2, 0, 1, 3))
    blocks_cot = jnp.transpose(cotangent, (2, 0, 1, 3))
    initial = (jnp.zeros((2, KB, FQ, PB), jnp.float32), jnp.zeros((PB, KB, FQ), jnp.float32))
    grads, block_outs = lax.scan(scan_step, initial, (blocks_in, blocks_cot))
    layer_out = jnp.transpose(block_outs[0], (1, 2, 0, 3))
    chan_cot = jnp.transpose(block_outs[1], (1, 2, 0, 3))
    total_cot = cotangent.astype(jnp.float32) + chan_cot
    mixed_tangent = rounded_values(total_cot * gating)
    straight_path = total_cot + total_cot * sequence_mixed * gating * (1.0 - gating) * gate_scale[:, :, None, None]
    section_tangent = rounded_values(jnp.einsum('vdy,medv->meyv', left_weight_matrix, mixed_tangent, precision=top_precision))
    left_factor_gradient = jnp.einsum('zueo,zuho->oeh', mixed_tangent, first_section, precision=top_precision)
    right_factor_gradient = jnp.einsum('advl,advu->vlu', section_tangent, input_tokens, precision=top_precision)
    token_input_gradient = straight_path + jnp.einsum('wmi,rfwm->rfwi', right_weight_matrix, section_tangent, precision=top_precision)
    return (layer_out, token_input_gradient, right_factor_gradient, left_factor_gradient, grads[0], grads[1])
```

```python
import jax
import jax.numpy as jnp
from jax import lax
from jax.experimental import pallas as pl
from jax.experimental.pallas import tpu as pltpu
from jax.sharding import PartitionSpec as P

F32 = jnp.float32
BF16 = jnp.bfloat16
PLANE = ("ch", "sub")


def dot(a, b, dims):
    return lax.dot_general(a, b, (dims, ((), ())), preferred_element_type=F32)


def channel_kernel(
    x_ref, cot_ref, up_ref, down_ref, mix_ref, shift_ref,
    back_ref, reduced_ref, up_grad_ref, down_grad_ref,
    x_all, cot_all, back_acc, reduced_acc,
):
    step = pl.program_id(0)
    shares, blocks, part = x_ref.shape[:3]

    @pl.when(step == 0)
    def _():
        for d in range(shares):
            x_all[:, d * part:(d + 1) * part, :] = x_ref[d]
            cot_all[:, d * part:(d + 1) * part, :] = cot_ref[d]
        back_acc[...] = jnp.zeros_like(back_acc)
        reduced_acc[...] = jnp.zeros_like(reduced_acc)

    def mix(g, j, k):
        col = (g * blocks + j) * blocks + k
        return mix_ref[:, col:col + 1]

    stacked = []
    for g in range(2):
        lifted = [dot(up_ref[g, k], x_all[k], ((1,), (0,))) for k in range(blocks)]
        rows = []
        for j in range(blocks):
            total = shift_ref[:, g * blocks + j:g * blocks + j + 1] + mix(g, j, 0) * lifted[0]
            for k in range(1, blocks):
                total = total + mix(g, j, k) * lifted[k]
            rows.append(total)
        stacked.append(rows)
    cots = [[], []]
    root = 0.7978845608028654
    for j in range(blocks):
        s0, s1 = stacked[0][j], stacked[1][j]
        square = s0 * s0
        t = jnp.tanh(root * (s0 + 0.044715 * (square * s0)))
        half = 0.5 * (1.0 + t)
        gelu = s0 * half
        slope = half + (0.5 * root) * s0 * (1.0 - t * t) * (1.0 + 3 * 0.044715 * square)
        hidden = (gelu * s1).astype(BF16)
        reduced_acc[j] += dot(down_ref[j], hidden, ((0,), (0,)))
        down_grad_ref[j] = dot(cot_all[j], hidden, ((1,), (1,))).astype(BF16)
        hidden_cot = dot(down_ref[j], cot_all[j], ((1,), (0,)))
        cots[0].append(hidden_cot * s1 * slope)
        cots[1].append(hidden_cot * gelu)
    for k in range(blocks):
        for g in range(2):
            total = mix(g, 0, k) * cots[g][0]
            for j in range(1, blocks):
                total = total + mix(g, j, k) * cots[g][j]
            lifted_cot = total.astype(BF16)
            back_acc[k] += dot(up_ref[g, k], lifted_cot, ((0,), (0,)))
            up_grad_ref[g, k] = dot(lifted_cot, x_all[k], ((1,), (1,))).astype(BF16)

    @pl.when(step == pl.num_programs(0) - 1)
    def _():
        for d in range(shares):
            back_ref[d] = back_acc[:, d * part:(d + 1) * part, :].astype(BF16)
            reduced_ref[d] = reduced_acc[:, d * part:(d + 1) * part, :].astype(BF16)


def channel_block(x, cot, up_first, up_second, up_shift, down_first):
    shares, blocks, part, tokens = x.shape
    chans = shares * part
    hidden = up_first.shape[2]
    if part % 16:
        x = jnp.swapaxes(x, 0, 1).reshape(1, blocks, chans, tokens)
        cot = jnp.swapaxes(cot, 0, 1).reshape(1, blocks, chans, tokens)
    tile = 128 if hidden % 128 == 0 else hidden
    down = jnp.transpose(down_first, (1, 2, 0))
    mix = jnp.transpose(up_second, (1, 0, 2, 3)).reshape(hidden, 2 * blocks * blocks).astype(F32)
    shift = jnp.transpose(up_shift, (2, 0, 1)).reshape(hidden, 2 * blocks)
    whole = pl.BlockSpec(x.shape, lambda i: (0, 0, 0, 0))
    back, reduced, up_grad, down_grad = pl.pallas_call(
        channel_kernel,
        grid=(hidden // tile,),
        in_specs=[
            whole,
            whole,
            pl.BlockSpec((2, blocks, tile, chans), lambda i: (0, 0, i, 0)),
            pl.BlockSpec((blocks, tile, chans), lambda i: (0, i, 0)),
            pl.BlockSpec((tile, 2 * blocks * blocks), lambda i: (i, 0)),
            pl.BlockSpec((tile, 2 * blocks), lambda i: (i, 0)),
        ],
        out_specs=[
            whole,
            whole,
            pl.BlockSpec((2, blocks, tile, chans), lambda i: (0, 0, i, 0)),
            pl.BlockSpec((blocks, chans, tile), lambda i: (0, 0, i)),
        ],
        out_shape=[
            jax.ShapeDtypeStruct(x.shape, BF16),
            jax.ShapeDtypeStruct(x.shape, BF16),
            jax.ShapeDtypeStruct((2, blocks, hidden, chans), BF16),
            jax.ShapeDtypeStruct((blocks, chans, hidden), BF16),
        ],
        scratch_shapes=[
            pltpu.VMEM((blocks, chans, tokens), BF16),
            pltpu.VMEM((blocks, chans, tokens), BF16),
            pltpu.VMEM((blocks, chans, tokens), F32),
            pltpu.VMEM((blocks, chans, tokens), F32),
        ],
        compiler_params=pltpu.CompilerParams(
            dimension_semantics=("arbitrary",), vmem_limit_bytes=50 * 1024 * 1024
        ),
        cost_estimate=pl.CostEstimate(
            flops=18 * blocks * hidden * chans * tokens,
            bytes_accessed=14 * 1024 * 1024,
            transcendentals=blocks * hidden * tokens,
        ),
    )(x, cot, up_first, down, mix, shift)
    if part % 16:
        back = jnp.swapaxes(back.reshape(blocks, shares, part, tokens), 0, 1)
        reduced = jnp.swapaxes(reduced.reshape(blocks, shares, part, tokens), 0, 1)
    return back, reduced, up_grad, down_grad


def pieces_sum(x, axes):
    moved = lax.all_to_all(x, axes, split_axis=0, concat_axis=0, tiled=True)
    return jnp.sum(moved.astype(F32), axis=0)


def ring_sum(x, axis, way):
    n = lax.axis_size(axis)
    me = lax.axis_index(axis)
    perm = [(i, (i + way) % n) for i in range(n)]
    rows = x.reshape(n, -1, x.shape[-1])

    def own(back):
        return lax.dynamic_index_in_dim(rows, (me - way * back) % n, 0, keepdims=False)

    held = own(1)
    for s in range(n - 1):
        held = (lax.ppermute(held, axis, perm).astype(F32) + own(s + 2).astype(F32)).astype(BF16)
    out = jnp.zeros(rows.shape, F32)
    out = lax.dynamic_update_index_in_dim(out, held.astype(F32), me, 0)
    for s in range(n - 1):
        held = lax.ppermute(held, axis, perm)
        out = lax.dynamic_update_index_in_dim(out, held.astype(F32), (me - way * (s + 1)) % n, 0)
    return out.reshape(x.shape)


def swap_sum(x):
    for axis in ("sub", "ch"):
        n = lax.axis_size(axis)
        bit = 1
        while bit < n:
            sent = x.astype(BF16)
            got = lax.ppermute(sent, axis, [(i, i ^ bit) for i in range(n)])
            x = sent.astype(F32) + got.astype(F32)
            bit *= 2
    return x


def per_device(
    tokens,
    gate_scale,
    gate_shift,
    sequence_right_factor,
    sequence_left_factor,
    up_first,
    up_second,
    up_shift,
    down_first,
    down_second,
    cotangent,
):
    blocks, part, _, length = tokens.shape
    rows = blocks * part
    n = lax.axis_size("seq")
    step = length // n
    right = sequence_right_factor[0]
    left = jnp.transpose(sequence_left_factor, (1, 2, 0)).astype(F32)
    flat = tokens.reshape(rows, length)
    upstream = cotangent.reshape(blocks, part, length)

    def to_positions(x):
        x = jnp.swapaxes(x.reshape(rows, n, step), 0, 1)
        return lax.all_to_all(x, "seq", split_axis=0, concat_axis=0, tiled=True)

    def to_blocks(x):
        x = lax.all_to_all(x, "seq", split_axis=0, concat_axis=0, tiled=True)
        return jnp.swapaxes(x, 0, 1).reshape(rows, length)

    section = dot(flat, right, ((1,), (1,))).astype(BF16)
    sections = to_positions(section)
    second = down_second.astype(F32)
    down_cot = jnp.stack(
        [
            sum(second[:, k, j, None] * upstream[k].astype(F32) for k in range(blocks))
            for j in range(blocks)
        ]
    ).astype(BF16)
    cot_all = lax.all_gather(down_cot, PLANE, axis=0)
    mixed = jnp.sum(left[:, :, None, :] * sections.astype(F32)[None], axis=1).astype(BF16)
    mixed_float = to_blocks(mixed).astype(F32)
    scale = gate_scale.reshape(rows, 1)
    shift = gate_shift.reshape(rows, 1)
    input_tokens = flat.astype(F32)
    gating = jax.nn.sigmoid(input_tokens * scale + shift)
    seq_out = (input_tokens + gating * mixed_float).astype(BF16)
    block_in = seq_out.reshape(blocks, part, length)
    x_all = lax.all_gather(block_in, PLANE, axis=0)
    back, reduced, up_grad, down_grad = channel_block(
        x_all, cot_all, up_first, up_second, up_shift, down_first
    )
    up_first_grad = ring_sum(up_grad, "seq", 1)
    down_first_grad = jnp.swapaxes(ring_sum(down_grad, "seq", -1), 0, 1)

    input_cot = pieces_sum(back, PLANE).reshape(rows, length)
    total_cot = cotangent.reshape(rows, length).astype(F32) + input_cot
    mixed_cot = (total_cot * gating).astype(BF16)
    straight = total_cot + total_cot * mixed_float * gating * (1.0 - gating) * scale
    cots = to_positions(mixed_cot).astype(F32)
    section_spread = jnp.sum(left[:, :, None, :] * cots[:, None], axis=0).astype(BF16)
    left_grad = jnp.sum(cots[:, None] * sections.astype(F32)[None], axis=2)
    section_cot = to_blocks(section_spread)
    right_grad = dot(section_cot, flat, ((0,), (0,)))
    token_grad = straight + dot(section_cot, right, ((1,), (0,)))

    sums = pieces_sum(reduced, PLANE)
    layer_out = jnp.stack(
        [
            block_in[k].astype(F32)
            + sum(second[:, k, j, None] * sums[j] for j in range(blocks))
            for k in range(blocks)
        ]
    ).astype(BF16)
    left_grad = jnp.transpose(swap_sum(left_grad), (2, 0, 1))
    right_grad = swap_sum(right_grad)
    return (
        layer_out.reshape(tokens.shape),
        token_grad.reshape(tokens.shape),
        right_grad[None],
        left_grad,
        up_first_grad,
        down_first_grad,
    )


def solution(mesh):
    placed = (
        P("grp", PLANE, "seq", None),
        P(None, PLANE),
        P(None, PLANE),
        P("seq", None, None),
        P("seq", None, None),
        P(None, None, PLANE, None),
        P(None, PLANE, None, None),
        P(None, None, PLANE),
        P(None, None, PLANE),
        P(PLANE, None, None),
        P("grp", PLANE, "seq", None),
    )
    return jax.shard_map(
        per_device,
        mesh=mesh,
        in_specs=placed,
        out_specs=(
            P("grp", PLANE, "seq", None),
            P("grp", PLANE, "seq", None),
            P(("grp", "seq"), None, None),
            P(("grp", "seq"), None, None),
            P("grp", None, PLANE, None),
            P("grp", None, PLANE),
        ),
        check_vma=False,
    )
```

```python
import jax
import jax.numpy as jnp
from jax import lax
from jax.experimental import pallas as pl
from jax.experimental.pallas import tpu as pltpu
from jax.sharding import PartitionSpec as P

F32 = jnp.float32
BF16 = jnp.bfloat16
PLANE = ("ch", "sub")


def dot(a, b, dims):
    return lax.dot_general(a, b, (dims, ((), ())), preferred_element_type=F32)


def channel_kernel(
    x_ref, cot_ref, up_ref, down_ref, mix_ref, shift_ref,
    back_ref, reduced_ref, up_grad_ref, down_grad_ref,
    x_all, cot_all, back_acc, reduced_acc,
):
    step = pl.program_id(0)
    shares, blocks, part = x_ref.shape[:3]

    @pl.when(step == 0)
    def _():
        for d in range(shares):
            x_all[:, d * part:(d + 1) * part, :] = x_ref[d]
            cot_all[:, d * part:(d + 1) * part, :] = cot_ref[d]
        back_acc[...] = jnp.zeros_like(back_acc)
        reduced_acc[...] = jnp.zeros_like(reduced_acc)

    def mix(g, j, k):
        col = (g * blocks + j) * blocks + k
        return mix_ref[:, col:col + 1]

    stacked = []
    for g in range(2):
        lifted = [dot(up_ref[g, k], x_all[k], ((1,), (0,))) for k in range(blocks)]
        rows = []
        for j in range(blocks):
            total = shift_ref[:, g * blocks + j:g * blocks + j + 1] + mix(g, j, 0) * lifted[0]
            for k in range(1, blocks):
                total = total + mix(g, j, k) * lifted[k]
            rows.append(total)
        stacked.append(rows)
    cots = [[], []]
    root = 0.7978845608028654
    for j in range(blocks):
        s0, s1 = stacked[0][j], stacked[1][j]
        square = s0 * s0
        t = jnp.tanh(root * (s0 + 0.044715 * (square * s0)))
        half = 0.5 * (1.0 + t)
        gelu = s0 * half
        slope = half + (0.5 * root) * s0 * (1.0 - t * t) * (1.0 + 3 * 0.044715 * square)
        hidden = (gelu * s1).astype(BF16)
        reduced_acc[j] += dot(down_ref[j], hidden, ((0,), (0,)))
        down_grad = dot(cot_all[j], hidden, ((1,), (1,)))
        chunk = down_grad_ref.shape[2]
        for d in range(down_grad_ref.shape[0]):
            down_grad_ref[d, j] = down_grad[d * chunk:(d + 1) * chunk].astype(BF16)
        hidden_cot = dot(down_ref[j], cot_all[j], ((1,), (0,)))
        cots[0].append(hidden_cot * s1 * slope)
        cots[1].append(hidden_cot * gelu)
    for k in range(blocks):
        for g in range(2):
            total = mix(g, 0, k) * cots[g][0]
            for j in range(1, blocks):
                total = total + mix(g, j, k) * cots[g][j]
            lifted_cot = total.astype(BF16)
            back_acc[k] += dot(up_ref[g, k], lifted_cot, ((0,), (0,)))
            up_grad_ref[g, k] = dot(lifted_cot, x_all[k], ((1,), (1,))).astype(BF16)

    @pl.when(step == pl.num_programs(0) - 1)
    def _():
        for d in range(shares):
            back_ref[d] = back_acc[:, d * part:(d + 1) * part, :].astype(BF16)
            reduced_ref[d] = reduced_acc[:, d * part:(d + 1) * part, :].astype(BF16)


def channel_block(x, cot, up_first, up_second, up_shift, down_first):
    shares, blocks, part, tokens = x.shape
    chans = shares * part
    hidden = up_first.shape[2]
    if part % 16:
        x = jnp.swapaxes(x, 0, 1).reshape(1, blocks, chans, tokens)
        cot = jnp.swapaxes(cot, 0, 1).reshape(1, blocks, chans, tokens)
    n = lax.axis_size("seq")
    chunks = n if (chans // n) % 16 == 0 else 1
    tile = 128 if hidden % 128 == 0 else hidden
    down = jnp.transpose(down_first, (1, 2, 0))
    mix = jnp.transpose(up_second, (1, 0, 2, 3)).reshape(hidden, 2 * blocks * blocks).astype(F32)
    shift = jnp.transpose(up_shift, (2, 0, 1)).reshape(hidden, 2 * blocks)
    whole = pl.BlockSpec(x.shape, lambda i: (0, 0, 0, 0))
    back, reduced, up_grad, down_grad = pl.pallas_call(
        channel_kernel,
        grid=(hidden // tile,),
        in_specs=[
            whole,
            whole,
            pl.BlockSpec((2, blocks, tile, chans), lambda i: (0, 0, i, 0)),
            pl.BlockSpec((blocks, tile, chans), lambda i: (0, i, 0)),
            pl.BlockSpec((tile, 2 * blocks * blocks), lambda i: (i, 0)),
            pl.BlockSpec((tile, 2 * blocks), lambda i: (i, 0)),
        ],
        out_specs=[
            whole,
            whole,
            pl.BlockSpec((2, blocks, tile, chans), lambda i: (0, 0, i, 0)),
            pl.BlockSpec((chunks, blocks, chans // chunks, tile), lambda i: (0, 0, 0, i)),
        ],
        out_shape=[
            jax.ShapeDtypeStruct(x.shape, BF16),
            jax.ShapeDtypeStruct(x.shape, BF16),
            jax.ShapeDtypeStruct((2, blocks, hidden, chans), BF16),
            jax.ShapeDtypeStruct((chunks, blocks, chans // chunks, hidden), BF16),
        ],
        scratch_shapes=[
            pltpu.VMEM((blocks, chans, tokens), BF16),
            pltpu.VMEM((blocks, chans, tokens), BF16),
            pltpu.VMEM((blocks, chans, tokens), F32),
            pltpu.VMEM((blocks, chans, tokens), F32),
        ],
        compiler_params=pltpu.CompilerParams(
            dimension_semantics=("arbitrary",), vmem_limit_bytes=50 * 1024 * 1024
        ),
        cost_estimate=pl.CostEstimate(
            flops=18 * blocks * hidden * chans * tokens,
            bytes_accessed=14 * 1024 * 1024,
            transcendentals=blocks * hidden * tokens,
        ),
    )(x, cot, up_first, down, mix, shift)
    if part % 16:
        back = jnp.swapaxes(back.reshape(blocks, shares, part, tokens), 0, 1)
        reduced = jnp.swapaxes(reduced.reshape(blocks, shares, part, tokens), 0, 1)
    if chunks != n:
        down_grad = jnp.swapaxes(down_grad.reshape(blocks, n, chans // n, hidden), 0, 1)
    return back, reduced, up_grad, down_grad


def pieces_sum(x, axes):
    moved = lax.all_to_all(x, axes, split_axis=0, concat_axis=0, tiled=True)
    return jnp.sum(moved.astype(F32), axis=0)


def ring_sums(parts, axis):
    n = lax.axis_size(axis)
    me = lax.axis_index(axis)
    perms = {way: [(i, (i + way) % n) for i in range(n)] for way in (1, -1)}

    def own(rows, way, back):
        return lax.dynamic_index_in_dim(rows, (me - way * back) % n, 0, keepdims=False)

    held = [own(rows, way, 1) for rows, way in parts]
    for s in range(n - 1):
        held = [
            (lax.ppermute(h, axis, perms[way]).astype(F32) + own(rows, way, s + 2).astype(F32)).astype(BF16)
            for h, (rows, way) in zip(held, parts)
        ]
    pieces = [[(me, h)] for h in held]
    for s in range(n - 1):
        held = [lax.ppermute(h, axis, perms[way]) for h, (_, way) in zip(held, parts)]
        for got, h, (_, way) in zip(pieces, held, parts):
            got.append(((me - way * (s + 1)) % n, h))
    return pieces


def swap_sum(x):
    for axis in ("sub", "ch"):
        n = lax.axis_size(axis)
        bit = 1
        while bit < n:
            sent = x.astype(BF16)
            got = lax.ppermute(sent, axis, [(i, i ^ bit) for i in range(n)])
            x = sent.astype(F32) + got.astype(F32)
            bit *= 2
    return x


def per_device(
    tokens,
    gate_scale,
    gate_shift,
    sequence_right_factor,
    sequence_left_factor,
    up_first,
    up_second,
    up_shift,
    down_first,
    down_second,
    cotangent,
):
    blocks, part, _, length = tokens.shape
    rows = blocks * part
    n = lax.axis_size("seq")
    step = length // n
    right = sequence_right_factor[0]
    left = jnp.transpose(sequence_left_factor, (1, 2, 0)).astype(F32)
    flat = tokens.reshape(rows, length)
    upstream = cotangent.reshape(blocks, part, length)

    def to_positions(x):
        x = jnp.swapaxes(x.reshape(rows, n, step), 0, 1)
        return lax.all_to_all(x, "seq", split_axis=0, concat_axis=0, tiled=True)

    def to_blocks(x):
        x = lax.all_to_all(x, "seq", split_axis=0, concat_axis=0, tiled=True)
        return jnp.swapaxes(x, 0, 1).reshape(rows, length)

    section = dot(flat, right, ((1,), (1,))).astype(BF16)
    sections = to_positions(section)
    second = down_second.astype(F32)
    down_cot = jnp.stack(
        [
            sum(second[:, k, j, None] * upstream[k].astype(F32) for k in range(blocks))
            for j in range(blocks)
        ]
    ).astype(BF16)
    cot_all = lax.all_gather(down_cot, PLANE, axis=0)
    mixed = jnp.sum(left[:, :, None, :] * sections.astype(F32)[None], axis=1).astype(BF16)
    mixed_float = to_blocks(mixed).astype(F32)
    scale = gate_scale.reshape(rows, 1)
    shift = gate_shift.reshape(rows, 1)
    input_tokens = flat.astype(F32)
    gating = jax.nn.sigmoid(input_tokens * scale + shift)
    seq_out = (input_tokens + gating * mixed_float).astype(BF16)
    block_in = seq_out.reshape(blocks, part, length)
    x_all = lax.all_gather(block_in, PLANE, axis=0)
    back, reduced, up_grad, down_grad = channel_block(
        x_all, cot_all, up_first, up_second, up_shift, down_first
    )
    up_rows = up_grad.reshape(2, n, -1, up_grad.shape[-1])
    gate_pieces, value_pieces, down_pieces = ring_sums(
        [(up_rows[0], 1), (up_rows[1], -1), (down_grad, 1)], "seq"
    )
    up_first_grad = jnp.zeros(up_rows.shape, F32)
    for s in range(n):
        for g, pieces in enumerate((gate_pieces, value_pieces)):
            at, piece = pieces[s]
            up_first_grad = lax.dynamic_update_slice(
                up_first_grad, piece.astype(F32)[None, None], (g, at, 0, 0)
            )
    up_first_grad = up_first_grad.reshape(up_grad.shape)
    share = down_grad.shape[2]
    down_first_grad = jnp.zeros((n * share,) + (blocks, down_grad.shape[3]), F32)
    for at, piece in down_pieces:
        turned = lax.optimization_barrier(jnp.swapaxes(piece, 0, 1).astype(F32))
        down_first_grad = lax.dynamic_update_slice(down_first_grad, turned, (at * share, 0, 0))

    input_cot = pieces_sum(back, PLANE).reshape(rows, length)
    total_cot = cotangent.reshape(rows, length).astype(F32) + input_cot
    mixed_cot = (total_cot * gating).astype(BF16)
    straight = total_cot + total_cot * mixed_float * gating * (1.0 - gating) * scale
    cots = to_positions(mixed_cot).astype(F32)
    section_spread = jnp.sum(left[:, :, None, :] * cots[:, None], axis=0).astype(BF16)
    left_grad = jnp.sum(cots[:, None] * sections.astype(F32)[None], axis=2)
    section_cot = to_blocks(section_spread)
    right_grad = dot(section_cot, flat, ((0,), (0,)))
    token_grad = straight + dot(section_cot, right, ((1,), (0,)))

    sums = pieces_sum(reduced, PLANE)
    layer_out = jnp.stack(
        [
            block_in[k].astype(F32)
            + sum(second[:, k, j, None] * sums[j] for j in range(blocks))
            for k in range(blocks)
        ]
    ).astype(BF16)
    left_grad = jnp.transpose(swap_sum(left_grad), (2, 0, 1))
    right_grad = swap_sum(right_grad)
    return (
        layer_out.reshape(tokens.shape),
        token_grad.reshape(tokens.shape),
        right_grad[None],
        left_grad,
        up_first_grad,
        down_first_grad,
    )


def solution(mesh):
    placed = (
        P("grp", PLANE, "seq", None),
        P(None, PLANE),
        P(None, PLANE),
        P("seq", None, None),
        P("seq", None, None),
        P(None, None, PLANE, None),
        P(None, PLANE, None, None),
        P(None, None, PLANE),
        P(None, None, PLANE),
        P(PLANE, None, None),
        P("grp", PLANE, "seq", None),
    )
    return jax.shard_map(
        per_device,
        mesh=mesh,
        in_specs=placed,
        out_specs=(
            P("grp", PLANE, "seq", None),
            P("grp", PLANE, "seq", None),
            P(("grp", "seq"), None, None),
            P(("grp", "seq"), None, None),
            P("grp", None, PLANE, None),
            P("grp", None, PLANE),
        ),
        check_vma=False,
    )
```

```python
import jax
import jax.numpy as jnp
from jax import lax
from jax.experimental import pallas as pl
from jax.experimental.pallas import tpu as pltpu
from jax.sharding import PartitionSpec as P

F32 = jnp.float32
BF16 = jnp.bfloat16
PLANE = ("ch", "sub")


def dot(a, b, dims):
    return lax.dot_general(a, b, (dims, ((), ())), preferred_element_type=F32)


def channel_kernel(
    x_ref, cot_ref, up_ref, down_ref, mix_ref, shift_ref,
    back_ref, reduced_ref, gate_grad_ref, value_grad_ref, down_grad_ref,
    x_all, cot_all, back_acc, reduced_acc,
):
    step = pl.program_id(0)
    shares, blocks, part = x_ref.shape[:3]

    @pl.when(step == 0)
    def _():
        for d in range(shares):
            x_all[:, d * part:(d + 1) * part, :] = x_ref[d]
            cot_all[:, d * part:(d + 1) * part, :] = cot_ref[d]
        back_acc[...] = jnp.zeros_like(back_acc)
        reduced_acc[...] = jnp.zeros_like(reduced_acc)

    def mix(g, j, k):
        col = (g * blocks + j) * blocks + k
        return mix_ref[:, col:col + 1]

    stacked = []
    for g in range(2):
        lifted = [dot(up_ref[g, k], x_all[k], ((1,), (0,))) for k in range(blocks)]
        rows = []
        for j in range(blocks):
            total = shift_ref[:, g * blocks + j:g * blocks + j + 1] + mix(g, j, 0) * lifted[0]
            for k in range(1, blocks):
                total = total + mix(g, j, k) * lifted[k]
            rows.append(total)
        stacked.append(rows)
    cots = [[], []]
    root = 0.7978845608028654
    for j in range(blocks):
        s0, s1 = stacked[0][j], stacked[1][j]
        square = s0 * s0
        t = jnp.tanh(root * (s0 + 0.044715 * (square * s0)))
        half = 0.5 * (1.0 + t)
        gelu = s0 * half
        slope = half + (0.5 * root) * s0 * (1.0 - t * t) * (1.0 + 3 * 0.044715 * square)
        hidden = (gelu * s1).astype(BF16)
        reduced_acc[j] += dot(down_ref[j], hidden, ((0,), (0,)))
        down_grad = dot(cot_all[j], hidden, ((1,), (1,)))
        chunk = down_grad_ref.shape[2]
        for d in range(down_grad_ref.shape[0]):
            down_grad_ref[d, j] = down_grad[d * chunk:(d + 1) * chunk].astype(BF16)
        hidden_cot = dot(down_ref[j], cot_all[j], ((1,), (0,)))
        cots[0].append(hidden_cot * s1 * slope)
        cots[1].append(hidden_cot * gelu)
    for k in range(blocks):
        for g in range(2):
            total = mix(g, 0, k) * cots[g][0]
            for j in range(1, blocks):
                total = total + mix(g, j, k) * cots[g][j]
            lifted_cot = total.astype(BF16)
            back_acc[k] += dot(up_ref[g, k], lifted_cot, ((0,), (0,)))
            grad_ref = (gate_grad_ref, value_grad_ref)[g]
            grad_ref[k] = dot(lifted_cot, x_all[k], ((1,), (1,))).astype(BF16)

    @pl.when(step == pl.num_programs(0) - 1)
    def _():
        for d in range(shares):
            back_ref[d] = back_acc[:, d * part:(d + 1) * part, :].astype(BF16)
            reduced_ref[d] = reduced_acc[:, d * part:(d + 1) * part, :].astype(BF16)


def channel_block(x, cot, up_first, up_second, up_shift, down_first):
    shares, blocks, part, tokens = x.shape
    chans = shares * part
    hidden = up_first.shape[2]
    if part % 16:
        x = jnp.swapaxes(x, 0, 1).reshape(1, blocks, chans, tokens)
        cot = jnp.swapaxes(cot, 0, 1).reshape(1, blocks, chans, tokens)
    n = lax.axis_size("seq")
    chunks = n if (chans // n) % 16 == 0 else 1
    tile = 128 if hidden % 128 == 0 else hidden
    down = jnp.transpose(down_first, (1, 2, 0))
    mix = jnp.transpose(up_second, (1, 0, 2, 3)).reshape(hidden, 2 * blocks * blocks).astype(F32)
    shift = jnp.transpose(up_shift, (2, 0, 1)).reshape(hidden, 2 * blocks)
    whole = pl.BlockSpec(x.shape, lambda i: (0, 0, 0, 0))
    back, reduced, gate_grad, value_grad, down_grad = pl.pallas_call(
        channel_kernel,
        grid=(hidden // tile,),
        in_specs=[
            whole,
            whole,
            pl.BlockSpec((2, blocks, tile, chans), lambda i: (0, 0, i, 0)),
            pl.BlockSpec((blocks, tile, chans), lambda i: (0, i, 0)),
            pl.BlockSpec((tile, 2 * blocks * blocks), lambda i: (i, 0)),
            pl.BlockSpec((tile, 2 * blocks), lambda i: (i, 0)),
        ],
        out_specs=[
            whole,
            whole,
            pl.BlockSpec((blocks, tile, chans), lambda i: (0, i, 0)),
            pl.BlockSpec((blocks, tile, chans), lambda i: (0, i, 0)),
            pl.BlockSpec((chunks, blocks, chans // chunks, tile), lambda i: (0, 0, 0, i)),
        ],
        out_shape=[
            jax.ShapeDtypeStruct(x.shape, BF16),
            jax.ShapeDtypeStruct(x.shape, BF16),
            jax.ShapeDtypeStruct((blocks, hidden, chans), BF16),
            jax.ShapeDtypeStruct((blocks, hidden, chans), BF16),
            jax.ShapeDtypeStruct((chunks, blocks, chans // chunks, hidden), BF16),
        ],
        scratch_shapes=[
            pltpu.VMEM((blocks, chans, tokens), BF16),
            pltpu.VMEM((blocks, chans, tokens), BF16),
            pltpu.VMEM((blocks, chans, tokens), F32),
            pltpu.VMEM((blocks, chans, tokens), F32),
        ],
        compiler_params=pltpu.CompilerParams(
            dimension_semantics=("arbitrary",), vmem_limit_bytes=50 * 1024 * 1024
        ),
        cost_estimate=pl.CostEstimate(
            flops=18 * blocks * hidden * chans * tokens,
            bytes_accessed=14 * 1024 * 1024,
            transcendentals=blocks * hidden * tokens,
        ),
    )(x, cot, up_first, down, mix, shift)
    if part % 16:
        back = jnp.swapaxes(back.reshape(blocks, shares, part, tokens), 0, 1)
        reduced = jnp.swapaxes(reduced.reshape(blocks, shares, part, tokens), 0, 1)
    if chunks != n:
        down_grad = jnp.swapaxes(down_grad.reshape(blocks, n, chans // n, hidden), 0, 1)
    return back, reduced, gate_grad, value_grad, down_grad


def pieces_sum(x, axes):
    moved = lax.all_to_all(x, axes, split_axis=0, concat_axis=0, tiled=True)
    return jnp.sum(moved.astype(F32), axis=0)


def after(values, *others):
    return lax.optimization_barrier((values, others))[0]


def own_rows(rows, axis, way, back):
    n = lax.axis_size(axis)
    at = (lax.axis_index(axis) - way * back) % n
    return lax.dynamic_index_in_dim(rows, at, 0, keepdims=False)


def ring_step(held, parts, axis):
    n = lax.axis_size(axis)
    return [
        lax.ppermute(h, axis, [(i, (i + way) % n) for i in range(n)])
        for h, (_, way) in zip(held, parts)
    ]


def ring_reduce(held, parts, axis, first, last):
    for s in range(first, last):
        held = [
            (h.astype(F32) + own_rows(rows, axis, way, s + 2).astype(F32)).astype(BF16)
            for h, (rows, way) in zip(ring_step(held, parts, axis), parts)
        ]
    return held


def ring_gather(pieces, parts, axis, first, last):
    n = lax.axis_size(axis)
    me = lax.axis_index(axis)
    held = [p[-1][1] for p in pieces]
    for s in range(first, last):
        held = ring_step(held, parts, axis)
        for got, h, (_, way) in zip(pieces, held, parts):
            got.append(((me - way * (s + 1)) % n, h))


def swap_sum(x):
    for axis in ("sub", "ch"):
        n = lax.axis_size(axis)
        bit = 1
        while bit < n:
            sent = x.astype(BF16)
            got = lax.ppermute(sent, axis, [(i, i ^ bit) for i in range(n)])
            x = sent.astype(F32) + got.astype(F32)
            bit *= 2
    return x


def per_device(
    tokens,
    gate_scale,
    gate_shift,
    sequence_right_factor,
    sequence_left_factor,
    up_first,
    up_second,
    up_shift,
    down_first,
    down_second,
    cotangent,
):
    blocks, part, _, length = tokens.shape
    rows = blocks * part
    n = lax.axis_size("seq")
    step = length // n
    right = sequence_right_factor[0]
    left = jnp.transpose(sequence_left_factor, (1, 2, 0)).astype(F32)
    flat = tokens.reshape(rows, length)
    upstream = cotangent.reshape(blocks, part, length)

    def to_positions(x):
        x = jnp.swapaxes(x.reshape(rows, n, step), 0, 1)
        return lax.all_to_all(x, "seq", split_axis=0, concat_axis=0, tiled=True)

    def to_blocks(x):
        x = lax.all_to_all(x, "seq", split_axis=0, concat_axis=0, tiled=True)
        return jnp.swapaxes(x, 0, 1).reshape(rows, length)

    section = dot(flat, right, ((1,), (1,))).astype(BF16)
    sections = to_positions(section)
    second = down_second.astype(F32)
    down_cot = jnp.stack(
        [
            sum(second[:, k, j, None] * upstream[k].astype(F32) for k in range(blocks))
            for j in range(blocks)
        ]
    ).astype(BF16)
    cot_all = lax.all_gather(down_cot, PLANE, axis=0)
    mixed = jnp.sum(left[:, :, None, :] * sections.astype(F32)[None], axis=1).astype(BF16)
    mixed_float = to_blocks(mixed).astype(F32)
    scale = gate_scale.reshape(rows, 1)
    shift = gate_shift.reshape(rows, 1)
    input_tokens = flat.astype(F32)
    gating = jax.nn.sigmoid(input_tokens * scale + shift)
    seq_out = (input_tokens + gating * mixed_float).astype(BF16)
    block_in = seq_out.reshape(blocks, part, length)
    x_all = lax.all_gather(block_in, PLANE, axis=0)
    back, reduced, gate_grad, value_grad, down_grad = channel_block(
        x_all, cot_all, up_first, up_second, up_shift, down_first
    )
    chans = gate_grad.shape[-1]
    parts = [
        (gate_grad.reshape(n, -1, chans), 1),
        (value_grad.reshape(n, -1, chans), -1),
        (down_grad, 1),
    ]
    held = [own_rows(rows_, "seq", way, 1) for rows_, way in parts]
    held = ring_reduce(held, parts, "seq", 0, 1)

    input_cot = pieces_sum(back, PLANE).reshape(rows, length)
    total_cot = cotangent.reshape(rows, length).astype(F32) + input_cot
    held = ring_reduce(after(held, input_cot), parts, "seq", 1, n - 1)
    mixed_cot = (total_cot * gating).astype(BF16)
    straight = total_cot + total_cot * mixed_float * gating * (1.0 - gating) * scale
    moved_cots = to_positions(mixed_cot)
    cots = moved_cots.astype(F32)
    held = after(held, moved_cots)
    reduced = after(reduced, moved_cots)
    pieces = [[(lax.axis_index("seq"), h)] for h in held]
    ring_gather(pieces, parts, "seq", 0, 1)
    section_spread = jnp.sum(left[:, :, None, :] * cots[:, None], axis=0).astype(BF16)
    left_grad = jnp.sum(cots[:, None] * sections.astype(F32)[None], axis=2)
    section_cot = to_blocks(section_spread)
    for p in pieces:
        p[-1] = (p[-1][0], after(p[-1][1], section_cot))
    ring_gather(pieces, parts, "seq", 1, n - 1)
    right_grad = dot(section_cot, flat, ((0,), (0,)))
    token_grad = straight + dot(section_cot, right, ((1,), (0,)))

    sums = pieces_sum(reduced, PLANE)
    layer_out = jnp.stack(
        [
            block_in[k].astype(F32)
            + sum(second[:, k, j, None] * sums[j] for j in range(blocks))
            for k in range(blocks)
        ]
    ).astype(BF16)
    up_first_grad = jnp.zeros((2,) + parts[0][0].shape, F32)
    for s in range(n):
        for g in range(2):
            at, piece = pieces[g][s]
            up_first_grad = lax.dynamic_update_slice(
                up_first_grad, piece.astype(F32)[None, None], (g, at, 0, 0)
            )
    up_first_grad = up_first_grad.reshape((2,) + gate_grad.shape)
    share = down_grad.shape[2]
    down_first_grad = jnp.zeros((n * share,) + (blocks, down_grad.shape[3]), F32)
    for at, piece in pieces[2]:
        turned = lax.optimization_barrier(jnp.swapaxes(piece, 0, 1).astype(F32))
        down_first_grad = lax.dynamic_update_slice(down_first_grad, turned, (at * share, 0, 0))
    left_grad = jnp.transpose(swap_sum(left_grad), (2, 0, 1))
    right_grad = swap_sum(right_grad)
    return (
        layer_out.reshape(tokens.shape),
        token_grad.reshape(tokens.shape),
        right_grad[None],
        left_grad,
        up_first_grad,
        down_first_grad,
    )


def solution(mesh):
    placed = (
        P("grp", PLANE, "seq", None),
        P(None, PLANE),
        P(None, PLANE),
        P("seq", None, None),
        P("seq", None, None),
        P(None, None, PLANE, None),
        P(None, PLANE, None, None),
        P(None, None, PLANE),
        P(None, None, PLANE),
        P(PLANE, None, None),
        P("grp", PLANE, "seq", None),
    )
    return jax.shard_map(
        per_device,
        mesh=mesh,
        in_specs=placed,
        out_specs=(
            P("grp", PLANE, "seq", None),
            P("grp", PLANE, "seq", None),
            P(("grp", "seq"), None, None),
            P(("grp", "seq"), None, None),
            P("grp", None, PLANE, None),
            P("grp", None, PLANE),
        ),
        check_vma=False,
    )
```
